32 devices in a mesh: dev: 32 (over z, y, x, core).
Axes of the slice: x: 2, y: 2, z: 4, core: 2. Of those that a mesh axis runs over, the one named last changes fastest.
Arguments:
- embeddings: bfloat16 [64, 128, 1280], P('dev')
- lengths: int32 [64], replicated, may hold values from 16 to 128, as said below
- pairs: int32 [32, 2], replicated, may hold values from 0 to 63, as said below
- labels: int32 [32], P('dev'), may hold values 0 or 1
- w_query: bfloat16 [1280, 1280], replicated, may hold values from -0.15625 to 0.15625
- w_key: bfloat16 [1280, 1280], replicated, may hold values from -0.15625 to 0.15625
- w_value: bfloat16 [1280, 1280], replicated, may hold values from -0.15625 to 0.15625
- w_out: bfloat16 [1280, 1280], replicated, may hold values from -0.15625 to 0.15625
- w_class: float32 [1280], replicated, may hold values from -4 to 4
Outputs:
- d_embeddings: float32 [64, 128, 1280], P('dev')
- d_weights: float32 [1280, 4, 1280], P('dev')
The draws below stay inside these ranges and needn't reach their ends.
Inputs may be any that keep to these rules, and one draw needn't show every extreme that they name: `pairs`: the two ids of a pair differ. `lengths`: some chain has exactly 128 residues.
All inputs are finite; a program needn't handle non-finite values. No bound on the sum of `labels` on one device may be relied on, other than what follows from the above.
Results may differ from the reference program's by a relative error of at most 0.013.
Values may be sent and summed in bfloat16 or wider, within the bound.
A program may use at most 192 MiB of HBM per device.

```python
import jax
import jax.numpy as jnp
from jax import lax

D = 1280
HEADS = 16
L = 128
PAIR_DEV = 1
CHAINS = 64
PAIRS = 32


def draw_embeddings(key, part):
    key = jax.random.fold_in(key, 11)
    first = jax.random.fold_in(key, 0)
    values = jnp.clip(jax.random.normal(first, (CHAINS, L, D), jnp.float32), -6.0, 6.0)
    return values.astype(jnp.bfloat16)


def draw_lengths(key, part):
    key = jax.random.fold_in(key, 5)
    first, second = jax.random.split(key)
    counts = jax.random.randint(first, (CHAINS,), L // 8, L + 1, jnp.int32)
    spot = jax.random.randint(second, (), 0, CHAINS, jnp.int32)
    return counts.at[spot].set(L)


def draw_pairs(key, part):
    key = jax.random.fold_in(key, 7)
    first, second = jax.random.split(key)
    left = jax.random.randint(first, (PAIRS,), 0, CHAINS, jnp.int32)
    offset = jax.random.randint(second, (PAIRS,), 1, CHAINS, jnp.int32)
    right = (left + offset) % CHAINS
    return jnp.stack([left, right], axis=1)


def set_ends(entries, rng, smallest, largest):
    longest = entries.shape.index(max(entries.shape))
    spots = []
    for shift in (0, 1):
        where = [jax.random.randint(jax.random.fold_in(rng, axis), (), 0, length) for axis, length in enumerate(entries.shape)]
        where[longest] = (where[longest] + shift) % entries.shape[longest]
        spots.append(tuple(where))
    return entries.at[spots[0]].set(smallest).at[spots[1]].set(largest)


def normal_values(stream_key, shape, deviation, reach, held_as=jnp.bfloat16):
    drawn = deviation * jax.random.normal(stream_key, shape, jnp.float32)
    return jnp.clip(drawn, min=-reach, max=reach).astype(held_as)


def setup_inputs(seed: int = 0) -> dict:
    splits = jax.random.split(jax.random.key(seed), 10)
    return {
        "embeddings": draw_embeddings(jax.random.fold_in(splits[9], 71), 0),
        "lengths": draw_lengths(jax.random.fold_in(splits[9], 71), 0),
        "pairs": draw_pairs(jax.random.fold_in(splits[9], 71), 0),
        "labels": set_ends((jax.random.randint(splits[3], (PAIRS,), 0, 2) < 1).astype(jnp.int32), jax.random.fold_in(splits[3], 1), 0, 1),
        "w_query": normal_values(splits[4], (D, D), D ** -0.5, 0.15625),
        "w_key": normal_values(splits[5], (D, D), D ** -0.5, 0.15625),
        "w_value": normal_values(splits[6], (D, D), D ** -0.5, 0.15625),
        "w_out": normal_values(splits[7], (D, D), D ** -0.5, 0.15625),
        "w_class": normal_values(splits[8], (D,), 1.0, 4.0, jnp.float32),
    }


def attend(query, keys, values, key_lens):
    npair, sides, length, width = query.shape
    head_dim = width // HEADS
    qh = query.reshape(npair, sides, length, HEADS, head_dim).astype(jnp.float32)
    kh = keys.reshape(npair, sides, length, HEADS, head_dim).astype(jnp.float32)
    vh = values.reshape(npair, sides, length, HEADS, head_dim).astype(jnp.float32)
    scores = jnp.einsum('psqhd,pskhd->pshqk', qh, kh) * head_dim ** (-0.5)
    slots = jnp.arange(length, dtype=jnp.int32)
    key_valid = slots[None, None, None, None, :] < key_lens[:, :, None, None, None]
    scores = jnp.where(key_valid, scores, -1000000000.0)
    scores = scores - lax.optimization_barrier(jnp.max(scores, axis=-1, keepdims=True))
    expo = jnp.exp(scores)
    probs = (expo / lax.optimization_barrier(jnp.sum(expo, axis=-1, keepdims=True))).astype(jnp.bfloat16)
    context = jnp.einsum('pshqk,pskhd->psqhd', probs.astype(jnp.float32), vh)
    return context.reshape(npair, sides, length, width).astype(jnp.bfloat16)

def forward_backward(chains, chain_lens, pair_labels, w_query, w_key, w_value, w_out, w_class):
    npair, sides, length, width = chains.shape
    flat_x = chains.reshape(-1, width)
    query = jnp.dot(flat_x, w_query, preferred_element_type=jnp.float32).astype(jnp.bfloat16).reshape(chains.shape)
    keys = jnp.dot(flat_x, w_key, preferred_element_type=jnp.float32).astype(jnp.bfloat16).reshape(chains.shape)
    values = jnp.dot(flat_x, w_value, preferred_element_type=jnp.float32).astype(jnp.bfloat16).reshape(chains.shape)
    other_lens = chain_lens[:, ::-1]

    def attention(q_in, k_in, v_in):
        return attend(q_in, k_in, v_in, other_lens)
    context, attention_back = jax.vjp(attention, query, keys[:, ::-1], values[:, ::-1])
    flat_ctx = context.reshape(-1, width)
    outputs = jnp.dot(flat_ctx, w_out, preferred_element_type=jnp.float32).reshape(chains.shape)
    slots = jnp.arange(length, dtype=jnp.int32)
    valid = (slots[None, None, :] < chain_lens[:, :, None]).astype(jnp.float32)
    lens_float = chain_lens.astype(jnp.float32)
    mixed = chains.astype(jnp.float32) + outputs
    pooled = lax.optimization_barrier(jnp.sum(mixed * valid[..., None], axis=2)) / lens_float[..., None]
    logits = lax.optimization_barrier(jnp.sum(w_class[None, :] * pooled[:, 0] * pooled[:, 1], axis=-1))
    slope = jax.nn.sigmoid(logits) - pair_labels.astype(jnp.float32)
    d_pooled = slope[:, None, None] * w_class[None, None, :] * pooled[:, ::-1]
    d_mixed = valid[..., None] * (d_pooled / lens_float[..., None])[:, :, None, :]
    d_out = d_mixed.astype(jnp.bfloat16).reshape(-1, width)
    d_ctx = lax.dot_general(d_out, w_out, (((1,), (1,)), ((), ())), preferred_element_type=jnp.float32)
    d_ctx = d_ctx.astype(jnp.bfloat16).reshape(chains.shape)
    d_query, d_keys_other, d_values_other = attention_back(d_ctx)
    d_keys = d_keys_other[:, ::-1]
    d_values = d_values_other[:, ::-1]
    grads_three = jnp.concatenate([d_query.reshape(-1, width), d_keys.reshape(-1, width), d_values.reshape(-1, width)], axis=1)
    stacked = jnp.concatenate([w_query, w_key, w_value], axis=1)
    back_in = lax.dot_general(grads_three, stacked, (((1,), (1,)), ((), ())), preferred_element_type=jnp.float32)
    d_input = d_mixed + back_in.reshape(chains.shape)
    return (d_input, flat_x, grads_three, flat_ctx, d_out)

def weight_grads(flat_x, grads_three, flat_ctx, d_out):
    upper = lax.dot_general(flat_x, grads_three, (((0,), (0,)), ((), ())), preferred_element_type=jnp.float32)
    lower = lax.dot_general(flat_ctx, d_out, (((0,), (0,)), ((), ())), preferred_element_type=jnp.float32)
    joined = jnp.concatenate([upper, lower], axis=1)
    return joined.reshape(flat_x.shape[1], 4, d_out.shape[1])

def reference(embeddings, lengths, pairs, labels, w_query, w_key, w_value, w_out, w_class):
    npairs = pairs.shape[0]
    blocks = npairs // PAIR_DEV
    pair_blocks = pairs.reshape(blocks, PAIR_DEV, 2)
    label_blocks = labels.reshape(blocks, PAIR_DEV)

    def step(carry, item):
        d_emb, d_w = carry
        ids, block_labels = item
        chains = jnp.take(embeddings, ids, axis=0)
        chain_lens = jnp.take(lengths, ids, axis=0)
        d_input, flat_x, grads_three, flat_ctx, d_out = forward_backward(chains, chain_lens, block_labels, w_query, w_key, w_value, w_out, w_class)
        d_w = d_w + weight_grads(flat_x, grads_three, flat_ctx, d_out)
        d_emb = d_emb.at[ids.reshape(-1)].add(d_input.reshape(-1, L, D))
        return ((d_emb, d_w), None)
    init = (jnp.zeros((embeddings.shape[0], L, D), jnp.float32), jnp.zeros((D, 4, D), jnp.float32))
    (d_emb, d_w), _ = lax.scan(step, init, (pair_blocks, label_blocks))
    return (d_emb, d_w)
```

```python
import functools

import jax
import jax.numpy as jnp
from jax import lax
from jax.experimental import pallas as pl
from jax.experimental.pallas import tpu as pltpu
from jax.sharding import PartitionSpec as P

HEADS = 16
BF = jnp.bfloat16
F32 = jnp.float32
NT = (((1,), (1,)), ((), ()))
TN = (((0,), (0,)), ((), ()))
NN = (((1,), (0,)), ((), ()))


def mm(a, b, dims=NN):
    return lax.dot_general(a, b, dims, preferred_element_type=F32)


def split(value, pieces):
    parts = []
    for _ in range(pieces):
        part = value.astype(BF)
        parts.append(part)
        value = value - part.astype(F32)
    return parts


def local_kernel(
    lens_ref, label_ref, x_ref, wq_ref, wk_ref, wv_ref, wo_ref, wc_ref,
    din_ref, dq_ref, dk_ref, small_ref,
    q_s, k_s, v_s, dv_s, p_s, cs_s, dqa_s, dka_s, dm_s,
):
    rows, width = x_ref.shape
    length = rows // 2
    hd = width // HEADS
    scale = hd ** (-0.5)
    step = 256
    x = x_ref[...]

    def project(n, carry):
        sl = pl.ds(pl.multiple_of(n * step, step), step)
        q_s[:, sl] = mm(x, wq_ref[:, sl]).astype(BF)
        k_s[:, sl] = mm(x, wk_ref[:, sl]).astype(BF)
        v_s[:, sl] = mm(x, wv_ref[:, sl]).astype(BF)
        return carry

    lax.fori_loop(0, width // step, project, 0)

    def window(h):
        first = (h * hd) // 128 * 128
        last = -(-(h * hd + hd) // 128) * 128
        return first, last

    def head_mask(h):
        first, last = window(h)
        lane = lax.broadcasted_iota(jnp.int32, (length, last - first), 1) + first
        return (lane >= h * hd) & (lane < h * hd + hd)

    def side(ref, s, first=0, last=width):
        return ref[s * length:(s + 1) * length, first:last]

    key_lane = lax.broadcasted_iota(jnp.int32, (length, length), 1)
    row_ids = lax.broadcasted_iota(jnp.int32, (length, 1), 0)
    for s in range(2):
        key_ok = key_lane < lens_ref[1 - s]
        live = (row_ids < lens_ref[s]).astype(F32)
        for h in range(HEADS):
            first, last = window(h)
            keys = side(k_s, 1 - s, first, last)
            keys = jnp.where(head_mask(h), keys, jnp.zeros_like(keys))
            scores = mm(side(q_s, s, first, last), keys, NT) * scale
            scores = jnp.where(key_ok, scores, -1000000000.0)
            expo = jnp.exp(scores - jnp.max(scores, axis=1, keepdims=True))
            probs = expo / jnp.sum(expo, axis=1, keepdims=True)
            p_s[s * HEADS + h] = probs
            rounded = probs.astype(BF).astype(F32)
            cs_s[s * HEADS + h:s * HEADS + h + 1, :] = jnp.sum(
                rounded * live, axis=0, keepdims=True
            )

    lane16 = lax.broadcasted_iota(jnp.int32, (HEADS, width), 1)
    head16 = lax.broadcasted_iota(jnp.int32, (HEADS, width), 0)
    own16 = (lane16 >= head16 * hd) & (lane16 < head16 * hd + hd)

    sum_x, ctx_sum, pieces = [], [], []
    for s in range(2):
        col_hi, col_lo = split(cs_s[s * HEADS:(s + 1) * HEADS, :], 2)
        other_v = side(v_s, 1 - s)
        full = mm(col_hi, other_v) + mm(col_lo, other_v)
        ctx = jnp.sum(jnp.where(own16, full, 0.0), axis=0, keepdims=True)
        ctx_sum.append(ctx)
        pieces += [part.astype(F32) for part in split(ctx, 3)]
        slot = lax.broadcasted_iota(jnp.int32, (8, length), 1)
        valid = (slot < lens_ref[s]).astype(F32).astype(BF)
        sum_x.append(mm(valid, side(x_ref, s))[0:1, :])
        other_x = side(x_ref, 1 - s)
        small_ref[s * HEADS:(s + 1) * HEADS, :] = (
            mm(col_hi, other_x) + mm(col_lo, other_x)
        ).astype(BF)
    zero = jnp.zeros((1, width), F32)
    stacked = jnp.concatenate(pieces + [zero, zero], axis=0).astype(BF)
    proj = mm(stacked, wo_ref[...])
    wc = wc_ref[...]
    pooled, lens = [], []
    for s in range(2):
        lens.append(jnp.full((1, 1), lens_ref[s], jnp.int32).astype(F32))
        out = proj[3 * s:3 * s + 1] + proj[3 * s + 1:3 * s + 2] + proj[3 * s + 2:3 * s + 3]
        pooled.append((sum_x[s] + out) / lens[s])
    logit = jnp.sum(wc * pooled[0] * pooled[1], axis=1, keepdims=True)
    label = jnp.full((1, 1), label_ref[0], jnp.int32).astype(F32)
    slope = 1.0 / (1.0 + jnp.exp(-logit)) - label
    d_mixed = [slope * wc * pooled[1 - s] / lens[s] for s in range(2)]
    d_rows = jnp.concatenate(d_mixed + [zero] * 6, axis=0)
    dm_s[...] = d_rows
    d_out = d_rows.astype(BF)
    d_ctx = mm(d_out, wo_ref[...], NT)
    tail = jnp.concatenate(
        ctx_sum + [d_out.astype(F32)[0:2], d_ctx[0:2], zero, zero], axis=0
    )
    small_ref[2 * HEADS:2 * HEADS + 8, :] = tail.astype(BF)

    dqa_s[...] = jnp.zeros_like(dqa_s)
    dka_s[...] = jnp.zeros_like(dka_s)
    for s in range(2):
        o = 1 - s
        grad = jnp.broadcast_to(d_ctx[s:s + 1], (HEADS, width))
        grad = jnp.where(own16, grad, 0.0).astype(BF)
        col_hi, col_lo = split(cs_s[s * HEADS:(s + 1) * HEADS, :], 2)
        dv_s[o * length:(o + 1) * length, :] = (
            mm(col_hi, grad, TN) + mm(col_lo, grad, TN)
        ).astype(BF)
        d_probs = mm(grad, side(v_s, o), NT).astype(BF).astype(F32)
        live = (row_ids < lens_ref[s]).astype(F32) * scale
        for h in range(HEADS):
            first, last = window(h)
            mask = head_mask(h)
            probs = p_s[s * HEADS + h]
            term = probs * d_probs[h:h + 1, :]
            total = jnp.sum(term, axis=1, keepdims=True)
            d_scores = ((term - probs * total) * live).astype(BF)
            keys = side(k_s, o, first, last)
            query = side(q_s, s, first, last)
            keys = jnp.where(mask, keys, jnp.zeros_like(keys))
            query = jnp.where(mask, query, jnp.zeros_like(query))
            dqa_s[s * length:(s + 1) * length, first:last] += mm(d_scores, keys)
            dka_s[o * length:(o + 1) * length, first:last] += mm(d_scores, query, TN)
    dq_ref[...] = dqa_s[...].astype(BF)
    dk_ref[...] = dka_s[...].astype(BF)

    def back(n, carry):
        sl = pl.ds(pl.multiple_of(n * step, step), step)
        total = mm(dq_ref[...], wq_ref[sl, :], NT)
        total = total + mm(dk_ref[...], wk_ref[sl, :], NT)
        total = total + mm(dv_s[...], wv_ref[sl, :], NT)
        for s in range(2):
            live = row_ids < lens_ref[s]
            mixed = jnp.where(live, dm_s[s:s + 1, sl], 0.0)
            din_ref[s * length:(s + 1) * length, sl] = (
                total[s * length:(s + 1) * length] + mixed
            ).astype(BF)
        return carry

    lax.fori_loop(0, width // step, back, 0)


def local_step(x, lens, label, wq, wk, wv, wo, wc):
    rows, width = x.shape
    length = rows // 2
    vmem = pl.BlockSpec(memory_space=pltpu.VMEM)
    smem = pl.BlockSpec(memory_space=pltpu.SMEM)
    like = jax.ShapeDtypeStruct((rows, width), BF)
    return pl.pallas_call(
        local_kernel,
        out_shape=(like, like, like, jax.ShapeDtypeStruct((2 * HEADS + 8, width), BF)),
        in_specs=[smem, smem] + [vmem] * 6,
        out_specs=(vmem,) * 4,
        scratch_shapes=[
            pltpu.VMEM((rows, width), BF),
            pltpu.VMEM((rows, width), BF),
            pltpu.VMEM((rows, width), BF),
            pltpu.VMEM((rows, width), BF),
            pltpu.VMEM((2 * HEADS, length, length), F32),
            pltpu.VMEM((2 * HEADS, length), F32),
            pltpu.VMEM((rows, width), F32),
            pltpu.VMEM((rows, width), F32),
            pltpu.VMEM((8, width), F32),
        ],
        compiler_params=pltpu.CompilerParams(vmem_limit_bytes=48 * 1024 * 1024),
        cost_estimate=pl.CostEstimate(
            flops=6 * 2 * rows * width * width,
            bytes_accessed=4 * 2 * width * width + 8 * 2 * rows * width,
            transcendentals=2 * HEADS * length * length,
        ),
    )(lens, label, x, wq, wk, wv, wo, wc.reshape(1, width))


def swap(value, n, bit):
    return lax.ppermute(value, "dev", [(i, i ^ (1 << bit)) for i in range(n)])


def halve(part, me, n, order):
    bits = (n // 2).bit_length() - 1
    cols = part.shape[-2:]
    part = part.reshape((2,) * bits + part.shape[1:])
    left = list(range(bits, 0, -1))
    for turn, bit in enumerate(order):
        axis = left.index(bit)
        mine = (me >> bit) & 1
        keep = lax.dynamic_index_in_dim(part, mine, axis, keepdims=False)
        send = lax.dynamic_index_in_dim(part, 1 - mine, axis, keepdims=False)
        got = swap(send, n, bit)
        part = keep.astype(F32) + got.astype(F32)
        if turn < len(order) - 1:
            part = part.astype(BF)
        left.pop(axis)
    return part.reshape((2,) + cols)


def shards(n, embeddings, lengths, pairs, labels, w_query, w_key, w_value, w_out, w_class):
    length = embeddings.shape[1]
    width = embeddings.shape[2]
    chain_total = lengths.shape[0]
    me = lax.axis_index("dev")
    spread = lax.all_to_all(embeddings, "dev", split_axis=1, concat_axis=0, tiled=True)
    slot_ids = pairs.reshape(-1)
    picked = spread.at[slot_ids].get(mode="promise_in_bounds")
    gathered = lax.all_to_all(picked, "dev", split_axis=0, concat_axis=1, tiled=True)
    x = gathered.reshape(2 * length, width)
    my_pair = lax.dynamic_index_in_dim(pairs, me, 0, keepdims=False)
    chain_lens = lengths.at[my_pair].get(mode="promise_in_bounds")

    x_other = swap(x, n, 0)
    d_input, d_query, d_keys, small = local_step(
        x, chain_lens, labels, w_query, w_key, w_value, w_out, w_class
    )

    core = me & 1
    first = core == 0
    own = jnp.where(first, d_query, d_keys)
    theirs = swap(jnp.where(first, d_keys, d_query), n, 0)
    factors = lax.all_gather(small, "dev", axis=0, tiled=False)

    chips = n // 2
    block = width // n
    bits = chips.bit_length() - 1
    orders = [list(range(1, bits + 1))]
    if bits >= 4:
        orders = [
            [1, 2] + list(range(3, bits + 1)),
            [2, 1] + list(range(3, bits + 1)),
            list(range(3, bits + 1)) + [1, 2],
        ]
    cuts = [0, width] if len(orders) == 1 else [0, 512, 1024, width]
    sums = []
    for order, lo, hi in zip(orders, cuts[:-1], cuts[1:]):
        part = mm(x, own[:, lo:hi], TN) + mm(x_other, theirs[:, lo:hi], TN)
        part = part.astype(BF).reshape(chips, 2, block, hi - lo)
        sums.append(halve(part, me, n, order))
    chip_sum = jnp.concatenate(sums, axis=-1)
    kept = lax.dynamic_index_in_dim(chip_sum, core, 0, keepdims=False)
    passed = lax.dynamic_index_in_dim(chip_sum, 1 - core, 0, keepdims=False)
    got = swap(passed.astype(BF), n, 0).astype(F32)
    d_wq = jnp.where(first, kept, got)
    d_wk = jnp.where(first, got, kept)

    slot_grads = d_input.reshape(2, length, width)
    by_rows = lax.all_to_all(slot_grads, "dev", split_axis=1, concat_axis=0, tiled=True)
    row_block = by_rows.shape[1]
    chain_index = jnp.arange(chain_total, dtype=jnp.int32)
    selector = (chain_index[:, None] == slot_ids[None, :]).astype(BF)
    summed = mm(selector, by_rows.reshape(slot_ids.shape[0], row_block * width)).astype(BF)
    summed = summed.reshape(chain_total, row_block, width)
    d_embeddings = lax.all_to_all(summed, "dev", split_axis=0, concat_axis=1, tiled=True)

    mine = lax.dynamic_slice_in_dim(factors, me * block, block, 2)
    tail = 2 * HEADS
    head_of = jnp.arange(width, dtype=jnp.int32) // (width // HEADS)
    own_head = head_of[None, :] == jnp.arange(HEADS, dtype=jnp.int32)[:, None]
    grads = factors[:, tail + 4:tail + 6]
    spread_grads = jnp.where(own_head, grads[:, :, None, :], jnp.zeros((), BF))
    d_wv = mm(
        mine[:, :tail].reshape(n * tail, block), spread_grads.reshape(n * tail, width), TN
    )
    d_wo = mm(
        mine[:, tail:tail + 2].reshape(n * 2, block),
        factors[:, tail + 2:tail + 4].reshape(n * 2, width),
        TN,
    )
    d_weights = jnp.stack([d_wq, d_wk, d_wv, d_wo], axis=1)
    return (d_embeddings.astype(F32), d_weights)


def solution(mesh):
    placed = (P("dev", None, None), P(), P(), P("dev"), P(), P(), P(), P(), P())
    return jax.shard_map(
        functools.partial(shards, mesh.shape["dev"]),
        mesh=mesh,
        in_specs=placed,
        out_specs=(P("dev", None, None), P("dev", None, None)),
        check_vma=False,
    )
```

```python
import functools

import jax
import jax.numpy as jnp
from jax import lax
from jax.experimental import pallas as pl
from jax.experimental.pallas import tpu as pltpu
from jax.sharding import PartitionSpec as P

HEADS = 16
BF = jnp.bfloat16
F32 = jnp.float32
NT = (((1,), (1,)), ((), ()))
TN = (((0,), (0,)), ((), ()))
NN = (((1,), (0,)), ((), ()))


def mm(a, b, dims=NN):
    return lax.dot_general(a, b, dims, preferred_element_type=F32)


def split(value, pieces):
    parts = []
    for _ in range(pieces):
        part = value.astype(BF)
        parts.append(part)
        value = value - part.astype(F32)
    return parts


def local_kernel(
    lens_ref, label_ref, core_ref, x_ref, wq_ref, wk_ref, wv_ref, wo_ref, wc_ref,
    din_ref, own_ref, other_ref, small_ref,
    q_s, k_s, v_s, dq_s, dk_s, dv_s, p_s, cs_s, dqa_s, dka_s, dm_s,
):
    rows, width = x_ref.shape
    length = rows // 2
    hd = width // HEADS
    scale = hd ** (-0.5)
    step = 256
    x = x_ref[...]

    def project(n, carry):
        sl = pl.ds(pl.multiple_of(n * step, step), step)
        q_s[:, sl] = mm(x, wq_ref[:, sl]).astype(BF)
        k_s[:, sl] = mm(x, wk_ref[:, sl]).astype(BF)
        v_s[:, sl] = mm(x, wv_ref[:, sl]).astype(BF)
        return carry

    lax.fori_loop(0, width // step, project, 0)

    def window(h):
        first = (h * hd) // 128 * 128
        last = -(-(h * hd + hd) // 128) * 128
        return first, last

    def head_mask(h):
        first, last = window(h)
        lane = lax.broadcasted_iota(jnp.int32, (length, last - first), 1) + first
        return (lane >= h * hd) & (lane < h * hd + hd)

    def side(ref, s, first=0, last=width):
        return ref[s * length:(s + 1) * length, first:last]

    key_lane = lax.broadcasted_iota(jnp.int32, (length, length), 1)
    row_ids = lax.broadcasted_iota(jnp.int32, (length, 1), 0)
    for s in range(2):
        key_ok = key_lane < lens_ref[1 - s]
        live = (row_ids < lens_ref[s]).astype(F32)
        for h in range(HEADS):
            first, last = window(h)
            keys = side(k_s, 1 - s, first, last)
            keys = jnp.where(head_mask(h), keys, jnp.zeros_like(keys))
            scores = mm(side(q_s, s, first, last), keys, NT) * scale
            scores = jnp.where(key_ok, scores, -1000000000.0)
            expo = jnp.exp(scores - jnp.max(scores, axis=1, keepdims=True))
            probs = expo / jnp.sum(expo, axis=1, keepdims=True)
            p_s[s * HEADS + h] = probs
            rounded = probs.astype(BF).astype(F32)
            cs_s[s * HEADS + h:s * HEADS + h + 1, :] = jnp.sum(
                rounded * live, axis=0, keepdims=True
            )

    lane16 = lax.broadcasted_iota(jnp.int32, (HEADS, width), 1)
    head16 = lax.broadcasted_iota(jnp.int32, (HEADS, width), 0)
    own16 = (lane16 >= head16 * hd) & (lane16 < head16 * hd + hd)

    sum_x, ctx_sum, pieces = [], [], []
    for s in range(2):
        col_hi, col_lo = split(cs_s[s * HEADS:(s + 1) * HEADS, :], 2)
        other_v = side(v_s, 1 - s)
        full = mm(col_hi, other_v) + mm(col_lo, other_v)
        ctx = jnp.sum(jnp.where(own16, full, 0.0), axis=0, keepdims=True)
        ctx_sum.append(ctx)
        pieces += [part.astype(F32) for part in split(ctx, 3)]
        slot = lax.broadcasted_iota(jnp.int32, (8, length), 1)
        valid = (slot < lens_ref[s]).astype(F32).astype(BF)
        sum_x.append(mm(valid, side(x_ref, s))[0:1, :])
        other_x = side(x_ref, 1 - s)
        small_ref[s * HEADS:(s + 1) * HEADS, :] = (
            mm(col_hi, other_x) + mm(col_lo, other_x)
        ).astype(BF)
    zero = jnp.zeros((1, width), F32)
    stacked = jnp.concatenate(pieces + [zero, zero], axis=0).astype(BF)
    proj = mm(stacked, wo_ref[...])
    wc = wc_ref[...]
    pooled, lens = [], []
    for s in range(2):
        lens.append(jnp.full((1, 1), lens_ref[s], jnp.int32).astype(F32))
        out = proj[3 * s:3 * s + 1] + proj[3 * s + 1:3 * s + 2] + proj[3 * s + 2:3 * s + 3]
        pooled.append((sum_x[s] + out) / lens[s])
    logit = jnp.sum(wc * pooled[0] * pooled[1], axis=1, keepdims=True)
    label = jnp.full((1, 1), label_ref[0], jnp.int32).astype(F32)
    slope = 1.0 / (1.0 + jnp.exp(-logit)) - label
    d_mixed = [slope * wc * pooled[1 - s] / lens[s] for s in range(2)]
    d_rows = jnp.concatenate(d_mixed + [zero] * 6, axis=0)
    dm_s[...] = d_rows
    d_out = d_rows.astype(BF)
    d_ctx = mm(d_out, wo_ref[...], NT)
    tail = jnp.concatenate(
        ctx_sum + [d_out.astype(F32)[0:2], d_ctx[0:2], zero, zero], axis=0
    )
    small_ref[2 * HEADS:2 * HEADS + 8, :] = tail.astype(BF)

    dqa_s[...] = jnp.zeros_like(dqa_s)
    dka_s[...] = jnp.zeros_like(dka_s)
    for s in range(2):
        o = 1 - s
        grad = jnp.broadcast_to(d_ctx[s:s + 1], (HEADS, width))
        grad = jnp.where(own16, grad, 0.0).astype(BF)
        col_hi, col_lo = split(cs_s[s * HEADS:(s + 1) * HEADS, :], 2)
        dv_s[o * length:(o + 1) * length, :] = (
            mm(col_hi, grad, TN) + mm(col_lo, grad, TN)
        ).astype(BF)
        d_probs = mm(grad, side(v_s, o), NT).astype(BF).astype(F32)
        live = (row_ids < lens_ref[s]).astype(F32) * scale
        for h in range(HEADS):
            first, last = window(h)
            mask = head_mask(h)
            probs = p_s[s * HEADS + h]
            term = probs * d_probs[h:h + 1, :]
            total = jnp.sum(term, axis=1, keepdims=True)
            d_scores = ((term - probs * total) * live).astype(BF)
            keys = side(k_s, o, first, last)
            query = side(q_s, s, first, last)
            keys = jnp.where(mask, keys, jnp.zeros_like(keys))
            query = jnp.where(mask, query, jnp.zeros_like(query))
            dqa_s[s * length:(s + 1) * length, first:last] += mm(d_scores, keys)
            dka_s[o * length:(o + 1) * length, first:last] += mm(d_scores, query, TN)
    dq_s[...] = dqa_s[...].astype(BF)
    dk_s[...] = dka_s[...].astype(BF)

    @pl.when(core_ref[0] == 0)
    def _():
        own_ref[...] = dq_s[...]
        other_ref[...] = dk_s[...]

    @pl.when(core_ref[0] == 1)
    def _():
        own_ref[...] = dk_s[...]
        other_ref[...] = dq_s[...]

    def back(n, carry):
        sl = pl.ds(pl.multiple_of(n * step, step), step)
        total = mm(dq_s[...], wq_ref[sl, :], NT)
        total = total + mm(dk_s[...], wk_ref[sl, :], NT)
        total = total + mm(dv_s[...], wv_ref[sl, :], NT)
        for s in range(2):
            live = row_ids < lens_ref[s]
            mixed = jnp.where(live, dm_s[s:s + 1, sl], 0.0)
            din_ref[s * length:(s + 1) * length, sl] = (
                total[s * length:(s + 1) * length] + mixed
            ).astype(BF)
        return carry

    lax.fori_loop(0, width // step, back, 0)


def local_step(x, lens, label, core, wq, wk, wv, wo, wc):
    rows, width = x.shape
    length = rows // 2
    vmem = pl.BlockSpec(memory_space=pltpu.VMEM)
    smem = pl.BlockSpec(memory_space=pltpu.SMEM)
    like = jax.ShapeDtypeStruct((rows, width), BF)
    return pl.pallas_call(
        local_kernel,
        out_shape=(like, like, like, jax.ShapeDtypeStruct((2 * HEADS + 8, width), BF)),
        in_specs=[smem] * 3 + [vmem] * 6,
        out_specs=(vmem,) * 4,
        scratch_shapes=[
            pltpu.VMEM((rows, width), BF),
            pltpu.VMEM((rows, width), BF),
            pltpu.VMEM((rows, width), BF),
            pltpu.VMEM((rows, width), BF),
            pltpu.VMEM((rows, width), BF),
            pltpu.VMEM((rows, width), BF),
            pltpu.VMEM((2 * HEADS, length, length), F32),
            pltpu.VMEM((2 * HEADS, length), F32),
            pltpu.VMEM((rows, width), F32),
            pltpu.VMEM((rows, width), F32),
            pltpu.VMEM((8, width), F32),
        ],
        compiler_params=pltpu.CompilerParams(vmem_limit_bytes=30 * 1024 * 1024),
        cost_estimate=pl.CostEstimate(
            flops=6 * 2 * rows * width * width,
            bytes_accessed=4 * 2 * width * width + 8 * 2 * rows * width,
            transcendentals=2 * HEADS * length * length,
        ),
    )(lens, label, core.reshape(1), x, wq, wk, wv, wo, wc.reshape(1, width))


def swap(value, n, bit):
    return lax.ppermute(value, "dev", [(i, i ^ (1 << bit)) for i in range(n)])


def halve_step(part, me, n, bit, left):
    axis = left.index(bit)
    mine = (me >> bit) & 1
    keep = lax.dynamic_index_in_dim(part, mine, axis, keepdims=False)
    send = lax.dynamic_index_in_dim(part, 1 - mine, axis, keepdims=False)
    return keep, swap(send, n, bit), [b for b in left if b != bit]


def chain_sums(by_rows, slot_ids, chain_total):
    slots, row_block, width = by_rows.shape
    chain_index = jnp.arange(chain_total, dtype=jnp.int32)
    selector = (chain_index[:, None] == slot_ids[None, :]).astype(BF)
    summed = mm(selector, by_rows.reshape(slots, row_block * width)).astype(BF)
    return summed.reshape(chain_total, row_block, width)


def shards(n, embeddings, lengths, pairs, labels, w_query, w_key, w_value, w_out, w_class):
    length = embeddings.shape[1]
    width = embeddings.shape[2]
    chain_total = lengths.shape[0]
    me = lax.axis_index("dev")
    spread = lax.all_to_all(embeddings, "dev", split_axis=1, concat_axis=0, tiled=True)
    slot_ids = pairs.reshape(-1)
    picked = spread.at[slot_ids].get(mode="promise_in_bounds")
    gathered = lax.all_to_all(picked, "dev", split_axis=0, concat_axis=1, tiled=True)
    x = gathered.reshape(2 * length, width)
    my_pair = lax.dynamic_index_in_dim(pairs, me, 0, keepdims=False)
    chain_lens = lengths.at[my_pair].get(mode="promise_in_bounds")

    x_both = jnp.concatenate([x, swap(x, n, 0)], axis=0)
    core = me & 1
    first = core == 0
    d_input, own, other, small = local_step(
        x, chain_lens, labels, core, w_query, w_key, w_value, w_out, w_class
    )
    own_both = jnp.concatenate([own, swap(other, n, 0)], axis=0)
    factors = lax.all_gather(small, "dev", axis=0, tiled=False)
    slot_grads = d_input.reshape(2, length, width)
    by_rows = lax.all_to_all(slot_grads, "dev", split_axis=1, concat_axis=0, tiled=True)

    chips = n // 2
    block = width // n
    bits = chips.bit_length() - 1
    straight = list(range(1, bits + 1))
    crossed = list(straight)
    for i in range(0, bits - 1, 2):
        crossed[i], crossed[i + 1] = straight[i + 1], straight[i]
    orders = [straight, crossed]
    half = width // 2
    parts = [
        mm(x_both, own_both[:, i * half:(i + 1) * half], TN)
        .astype(BF)
        .reshape((2,) * bits + (2, block, half))
        for i in range(2)
    ]
    lefts = [straight[::-1]] * 2
    for turn in range(bits):
        kept, came = [], []
        for i in range(2):
            keep, got, lefts[i] = halve_step(parts[i], me, n, orders[i][turn], lefts[i])
            kept.append(keep)
            came.append(got)
        if turn == 0:
            came[0], came[1], by_rows = lax.optimization_barrier((came[0], came[1], by_rows))
            summed = chain_sums(by_rows, slot_ids, chain_total)
        elif turn == 1:
            came[0], came[1], summed = lax.optimization_barrier((came[0], came[1], summed))
        else:
            came = list(lax.optimization_barrier(tuple(came)))
        parts = [k.astype(F32) + g.astype(F32) for k, g in zip(kept, came)]
        if turn < bits - 1:
            parts = [part.astype(BF) for part in parts]
    chip_sum = jnp.concatenate(parts, axis=-1)
    kept = lax.dynamic_index_in_dim(chip_sum, core, 0, keepdims=False)
    passed = lax.dynamic_index_in_dim(chip_sum, 1 - core, 0, keepdims=False)
    got = swap(passed.astype(BF), n, 0).astype(F32)
    d_wq = jnp.where(first, kept, got)
    d_wk = jnp.where(first, got, kept)

    d_embeddings = lax.all_to_all(summed, "dev", split_axis=0, concat_axis=1, tiled=True)

    column = jnp.arange(width, dtype=jnp.int32)[:, None]
    pick = (column == me * block + jnp.arange(block, dtype=jnp.int32)[None, :]).astype(BF)
    mine = mm(factors.reshape(-1, width), pick).astype(BF).reshape(n, -1, block)
    tail = 2 * HEADS
    head_of = jnp.arange(width, dtype=jnp.int32) // (width // HEADS)
    own_head = head_of[None, :] == jnp.arange(HEADS, dtype=jnp.int32)[:, None]
    grads = factors[:, tail + 4:tail + 6]
    spread_grads = jnp.where(own_head, grads[:, :, None, :], jnp.zeros((), BF))
    d_wv = mm(
        mine[:, :tail].reshape(n * tail, block), spread_grads.reshape(n * tail, width), TN
    )
    d_wo = mm(
        mine[:, tail:tail + 2].reshape(n * 2, block),
        factors[:, tail + 2:tail + 4].reshape(n * 2, width),
        TN,
    )
    d_weights = jnp.stack([d_wq, d_wk, d_wv, d_wo], axis=1)
    return (d_embeddings.astype(F32), d_weights)


def solution(mesh):
    placed = (P("dev", None, None), P(), P(), P("dev"), P(), P(), P(), P(), P())
    return jax.shard_map(
        functools.partial(shards, mesh.shape["dev"]),
        mesh=mesh,
        in_specs=placed,
        out_specs=(P("dev", None, None), P("dev", None, None)),
        check_vma=False,
    )
```

```python
import functools

import jax
import jax.numpy as jnp
from jax import lax
from jax.experimental import pallas as pl
from jax.experimental.pallas import tpu as pltpu
from jax.sharding import PartitionSpec as P

HEADS = 16
BF = jnp.bfloat16
F32 = jnp.float32
NT = (((1,), (1,)), ((), ()))
TN = (((0,), (0,)), ((), ()))
NN = (((1,), (0,)), ((), ()))


def mm(a, b, dims=NN):
    return lax.dot_general(a, b, dims, preferred_element_type=F32)


def split(value, pieces):
    parts = []
    for _ in range(pieces):
        part = value.astype(BF)
        parts.append(part)
        value = value - part.astype(F32)
    return parts


def local_kernel(
    lens_ref, label_ref, core_ref, x_ref, wq_hbm, wk_hbm, wv_hbm, wo_hbm, wc_ref,
    din_ref, own_ref, other_ref, small_ref,
    wq_ref, wk_ref, wv_ref, wo_ref, w_sems,
    q_s, k_s, v_s, dq_s, dk_s, dv_s, p_s, cs_s, dqa_s, dka_s, dm_s,
):
    rows, width = x_ref.shape
    length = rows // 2
    hd = width // HEADS
    scale = hd ** (-0.5)
    step = 256
    sources = (wq_hbm, wk_hbm, wv_hbm, wo_hbm)
    held = (wq_ref, wk_ref, wv_ref, wo_ref)
    loads = [
        pltpu.make_async_copy(source, place, w_sems.at[i])
        for i, (source, place) in enumerate(zip(sources, held))
    ]
    for load in loads:
        load.start()
    x = x_ref[...]
    for load, weight, result in zip(loads, held, (q_s, k_s, v_s)):
        load.wait()

        def project(n, carry, weight=weight, result=result):
            sl = pl.ds(pl.multiple_of(n * step, step), step)
            result[:, sl] = mm(x, weight[:, sl]).astype(BF)
            return carry

        lax.fori_loop(0, width // step, project, 0)

    def window(h):
        first = (h * hd) // 128 * 128
        last = -(-(h * hd + hd) // 128) * 128
        return first, last

    def head_mask(h):
        first, last = window(h)
        lane = lax.broadcasted_iota(jnp.int32, (length, last - first), 1) + first
        return (lane >= h * hd) & (lane < h * hd + hd)

    def side(ref, s, first=0, last=width):
        return ref[s * length:(s + 1) * length, first:last]

    key_lane = lax.broadcasted_iota(jnp.int32, (length, length), 1)
    row_ids = lax.broadcasted_iota(jnp.int32, (length, 1), 0)
    for s in range(2):
        key_ok = key_lane < lens_ref[1 - s]
        live = (row_ids < lens_ref[s]).astype(F32)
        for h in range(HEADS):
            first, last = window(h)
            keys = side(k_s, 1 - s, first, last)
            keys = jnp.where(head_mask(h), keys, jnp.zeros_like(keys))
            scores = mm(side(q_s, s, first, last), keys, NT) * scale
            scores = jnp.where(key_ok, scores, -1000000000.0)
            expo = jnp.exp(scores - jnp.max(scores, axis=1, keepdims=True))
            probs = expo / jnp.sum(expo, axis=1, keepdims=True)
            p_s[s * HEADS + h] = probs
            rounded = probs.astype(BF).astype(F32)
            cs_s[s * HEADS + h:s * HEADS + h + 1, :] = jnp.sum(
                rounded * live, axis=0, keepdims=True
            )

    loads[3].wait()
    lane16 = lax.broadcasted_iota(jnp.int32, (HEADS, width), 1)
    head16 = lax.broadcasted_iota(jnp.int32, (HEADS, width), 0)
    own16 = (lane16 >= head16 * hd) & (lane16 < head16 * hd + hd)

    sum_x, ctx_sum, pieces = [], [], []
    for s in range(2):
        col_hi, col_lo = split(cs_s[s * HEADS:(s + 1) * HEADS, :], 2)
        other_v = side(v_s, 1 - s)
        full = mm(col_hi, other_v) + mm(col_lo, other_v)
        ctx = jnp.sum(jnp.where(own16, full, 0.0), axis=0, keepdims=True)
        ctx_sum.append(ctx)
        pieces += [part.astype(F32) for part in split(ctx, 3)]
        slot = lax.broadcasted_iota(jnp.int32, (8, length), 1)
        valid = (slot < lens_ref[s]).astype(F32).astype(BF)
        sum_x.append(mm(valid, side(x_ref, s))[0:1, :])
        other_x = side(x_ref, 1 - s)
        small_ref[s * HEADS:(s + 1) * HEADS, :] = (
            mm(col_hi, other_x) + mm(col_lo, other_x)
        ).astype(BF)
    zero = jnp.zeros((1, width), F32)
    stacked = jnp.concatenate(pieces + [zero, zero], axis=0).astype(BF)
    proj = mm(stacked, wo_ref[...])
    wc = wc_ref[...]
    pooled, lens = [], []
    for s in range(2):
        lens.append(jnp.full((1, 1), lens_ref[s], jnp.int32).astype(F32))
        out = proj[3 * s:3 * s + 1] + proj[3 * s + 1:3 * s + 2] + proj[3 * s + 2:3 * s + 3]
        pooled.append((sum_x[s] + out) / lens[s])
    logit = jnp.sum(wc * pooled[0] * pooled[1], axis=1, keepdims=True)
    label = jnp.full((1, 1), label_ref[0], jnp.int32).astype(F32)
    slope = 1.0 / (1.0 + jnp.exp(-logit)) - label
    d_mixed = [slope * wc * pooled[1 - s] / lens[s] for s in range(2)]
    d_rows = jnp.concatenate(d_mixed + [zero] * 6, axis=0)
    dm_s[...] = d_rows
    d_out = d_rows.astype(BF)
    d_ctx = mm(d_out, wo_ref[...], NT)
    tail = jnp.concatenate(
        ctx_sum + [d_out.astype(F32)[0:2], d_ctx[0:2], zero, zero], axis=0
    )
    small_ref[2 * HEADS:2 * HEADS + 8, :] = tail.astype(BF)

    dqa_s[...] = jnp.zeros_like(dqa_s)
    dka_s[...] = jnp.zeros_like(dka_s)
    for s in range(2):
        o = 1 - s
        grad = jnp.broadcast_to(d_ctx[s:s + 1], (HEADS, width))
        grad = jnp.where(own16, grad, 0.0).astype(BF)
        col_hi, col_lo = split(cs_s[s * HEADS:(s + 1) * HEADS, :], 2)
        dv_s[o * length:(o + 1) * length, :] = (
            mm(col_hi, grad, TN) + mm(col_lo, grad, TN)
        ).astype(BF)
        d_probs = mm(grad, side(v_s, o), NT).astype(BF).astype(F32)
        live = (row_ids < lens_ref[s]).astype(F32) * scale
        for h in range(HEADS):
            first, last = window(h)
            mask = head_mask(h)
            probs = p_s[s * HEADS + h]
            term = probs * d_probs[h:h + 1, :]
            total = jnp.sum(term, axis=1, keepdims=True)
            d_scores = ((term - probs * total) * live).astype(BF)
            keys = side(k_s, o, first, last)
            query = side(q_s, s, first, last)
            keys = jnp.where(mask, keys, jnp.zeros_like(keys))
            query = jnp.where(mask, query, jnp.zeros_like(query))
            dqa_s[s * length:(s + 1) * length, first:last] += mm(d_scores, keys)
            dka_s[o * length:(o + 1) * length, first:last] += mm(d_scores, query, TN)
    dq_s[...] = dqa_s[...].astype(BF)
    dk_s[...] = dka_s[...].astype(BF)

    @pl.when(core_ref[0] == 0)
    def _():
        own_ref[...] = dq_s[...]
        other_ref[...] = dk_s[...]

    @pl.when(core_ref[0] == 1)
    def _():
        own_ref[...] = dk_s[...]
        other_ref[...] = dq_s[...]

    def back(n, carry):
        sl = pl.ds(pl.multiple_of(n * step, step), step)
        total = mm(dq_s[...], wq_ref[sl, :], NT)
        total = total + mm(dk_s[...], wk_ref[sl, :], NT)
        total = total + mm(dv_s[...], wv_ref[sl, :], NT)
        for s in range(2):
            live = row_ids < lens_ref[s]
            mixed = jnp.where(live, dm_s[s:s + 1, sl], 0.0)
            din_ref[s * length:(s + 1) * length, sl] = (
                total[s * length:(s + 1) * length] + mixed
            ).astype(BF)
        return carry

    lax.fori_loop(0, width // step, back, 0)


def local_step(x, lens, label, core, wq, wk, wv, wo, wc):
    rows, width = x.shape
    length = rows // 2
    vmem = pl.BlockSpec(memory_space=pltpu.VMEM)
    smem = pl.BlockSpec(memory_space=pltpu.SMEM)
    like = jax.ShapeDtypeStruct((rows, width), BF)
    return pl.pallas_call(
        local_kernel,
        out_shape=(like, like, like, jax.ShapeDtypeStruct((2 * HEADS + 8, width), BF)),
        in_specs=[smem] * 3 + [vmem] + [pl.BlockSpec(memory_space=pl.ANY)] * 4 + [vmem],
        out_specs=(vmem,) * 4,
        scratch_shapes=[
            pltpu.VMEM((width, width), BF),
            pltpu.VMEM((width, width), BF),
            pltpu.VMEM((width, width), BF),
            pltpu.VMEM((width, width), BF),
            pltpu.SemaphoreType.DMA((4,)),
            pltpu.VMEM((rows, width), BF),
            pltpu.VMEM((rows, width), BF),
            pltpu.VMEM((rows, width), BF),
            pltpu.VMEM((rows, width), BF),
            pltpu.VMEM((rows, width), BF),
            pltpu.VMEM((rows, width), BF),
            pltpu.VMEM((2 * HEADS, length, length), F32),
            pltpu.VMEM((2 * HEADS, length), F32),
            pltpu.VMEM((rows, width), F32),
            pltpu.VMEM((rows, width), F32),
            pltpu.VMEM((8, width), F32),
        ],
        compiler_params=pltpu.CompilerParams(vmem_limit_bytes=56 * 1024 * 1024),
        cost_estimate=pl.CostEstimate(
            flops=6 * 2 * rows * width * width,
            bytes_accessed=4 * 2 * width * width + 8 * 2 * rows * width,
            transcendentals=2 * HEADS * length * length,
        ),
    )(lens, label, core.reshape(1), x, wq, wk, wv, wo, wc.reshape(1, width))


def swap(value, n, bit):
    return lax.ppermute(value, "dev", [(i, i ^ (1 << bit)) for i in range(n)])


def halve_step(part, me, n, bit, left):
    axis = left.index(bit)
    mine = (me >> bit) & 1
    keep = lax.dynamic_index_in_dim(part, mine, axis, keepdims=False)
    send = lax.dynamic_index_in_dim(part, 1 - mine, axis, keepdims=False)
    return keep, swap(send, n, bit), [b for b in left if b != bit]


def chain_sums(by_rows, slot_ids, chain_total):
    slots, row_block, width = by_rows.shape
    chain_index = jnp.arange(chain_total, dtype=jnp.int32)
    selector = (chain_index[:, None] == slot_ids[None, :]).astype(BF)
    summed = mm(selector, by_rows.reshape(slots, row_block * width)).astype(BF)
    return summed.reshape(chain_total, row_block, width)


def factor_grads(factors, me, n):
    width = factors.shape[2]
    block = width // n
    tail = 2 * HEADS
    column = jnp.arange(width, dtype=jnp.int32)[:, None]
    pick = (column == me * block + jnp.arange(block, dtype=jnp.int32)[None, :]).astype(BF)
    mine = mm(factors.reshape(-1, width), pick).astype(BF).reshape(n, -1, block)
    head_of = jnp.arange(width, dtype=jnp.int32) // (width // HEADS)
    own_head = head_of[None, :] == jnp.arange(HEADS, dtype=jnp.int32)[:, None]
    grads = factors[:, tail + 4:tail + 6]
    spread_grads = jnp.where(own_head, grads[:, :, None, :], jnp.zeros((), BF))
    d_wv = mm(
        mine[:, :tail].reshape(n * tail, block), spread_grads.reshape(n * tail, width), TN
    )
    d_wo = mm(
        mine[:, tail:tail + 2].reshape(n * 2, block),
        factors[:, tail + 2:tail + 4].reshape(n * 2, width),
        TN,
    )
    return d_wv, d_wo


def shards(n, embeddings, lengths, pairs, labels, w_query, w_key, w_value, w_out, w_class):
    length = embeddings.shape[1]
    width = embeddings.shape[2]
    chain_total = lengths.shape[0]
    me = lax.axis_index("dev")
    spread = lax.all_to_all(embeddings, "dev", split_axis=1, concat_axis=0, tiled=True)
    slot_ids = pairs.reshape(-1)
    picked = spread.at[slot_ids].get(mode="promise_in_bounds")
    gathered = lax.all_to_all(picked, "dev", split_axis=0, concat_axis=1, tiled=True)
    x = gathered.reshape(2 * length, width)
    my_pair = lax.dynamic_index_in_dim(pairs, me, 0, keepdims=False)
    chain_lens = lengths.at[my_pair].get(mode="promise_in_bounds")

    x_both = jnp.concatenate([x, swap(x, n, 0)], axis=0)
    core = me & 1
    first = core == 0
    d_input, own, other, small = local_step(
        x, chain_lens, labels, core, w_query, w_key, w_value, w_out, w_class
    )
    own_both = jnp.concatenate([own, swap(other, n, 0)], axis=0)
    factors = lax.all_gather(small, "dev", axis=0, tiled=False)
    slot_grads = d_input.reshape(2, length, width)
    by_rows = lax.all_to_all(slot_grads, "dev", split_axis=1, concat_axis=0, tiled=True)

    chips = n // 2
    block = width // n
    bits = chips.bit_length() - 1
    straight = list(range(1, bits + 1))
    crossed = list(straight)
    for i in range(0, bits - 1, 2):
        crossed[i], crossed[i + 1] = straight[i + 1], straight[i]
    orders = [straight, crossed]
    half = width // 2
    parts = [
        mm(x_both, own_both[:, i * half:(i + 1) * half], TN)
        .astype(BF)
        .reshape((2,) * bits + (2, block, half))
        for i in range(2)
    ]
    lefts = [straight[::-1]] * 2
    for turn in range(bits):
        kept, came = [], []
        for i in range(2):
            keep, got, lefts[i] = halve_step(parts[i], me, n, orders[i][turn], lefts[i])
            kept.append(keep)
            came.append(got)
        if turn == 0:
            summed = chain_sums(by_rows, slot_ids, chain_total)
            came[0], came[1], summed = lax.optimization_barrier((came[0], came[1], summed))
            d_embeddings = lax.all_to_all(
                summed, "dev", split_axis=0, concat_axis=1, tiled=True
            )
        elif turn == 1:
            came[0], came[1], d_embeddings = lax.optimization_barrier(
                (came[0], came[1], d_embeddings)
            )
            d_embeddings = d_embeddings.astype(F32)
            small_grads = factor_grads(factors, me, n)
        elif turn == 2:
            came[0], came[1], d_embeddings, small_grads = lax.optimization_barrier(
                (came[0], came[1], d_embeddings, small_grads)
            )
        else:
            came = list(lax.optimization_barrier(tuple(came)))
        parts = [k.astype(F32) + g.astype(F32) for k, g in zip(kept, came)]
        if turn < bits - 1:
            parts = [part.astype(BF) for part in parts]
    chip_sum = jnp.concatenate(parts, axis=-1)
    kept = lax.dynamic_index_in_dim(chip_sum, core, 0, keepdims=False)
    passed = lax.dynamic_index_in_dim(chip_sum, 1 - core, 0, keepdims=False)
    got = swap(passed.astype(BF), n, 0).astype(F32)
    d_wq = jnp.where(first, kept, got)
    d_wk = jnp.where(first, got, kept)

    d_weights = jnp.stack([d_wq, d_wk, small_grads[0], small_grads[1]], axis=1)
    return (d_embeddings, d_weights)


def solution(mesh):
    placed = (P("dev", None, None), P(), P(), P("dev"), P(), P(), P(), P(), P())
    return jax.shard_map(
        functools.partial(shards, mesh.shape["dev"]),
        mesh=mesh,
        in_specs=placed,
        out_specs=(P("dev", None, None), P("dev", None, None)),
        check_vma=False,
    )
```

```python
import functools

import jax
import jax.numpy as jnp
from jax import lax
from jax.experimental import pallas as pl
from jax.experimental.pallas import tpu as pltpu
from jax.sharding import PartitionSpec as P

HEADS = 16
BF = jnp.bfloat16
F32 = jnp.float32
NT = (((1,), (1,)), ((), ()))
TN = (((0,), (0,)), ((), ()))
NN = (((1,), (0,)), ((), ()))


def mm(a, b, dims=NN):
    return lax.dot_general(a, b, dims, preferred_element_type=F32)


def split(value, pieces):
    parts = []
    for _ in range(pieces):
        part = value.astype(BF)
        parts.append(part)
        value = value - part.astype(F32)
    return parts


def local_kernel(
    lens_ref, label_ref, core_ref, x_ref, wq_hbm, wk_hbm, wv_hbm, wo_hbm, wc_ref,
    din_ref, own_ref, other_ref, small_ref,
    wq_ref, wk_ref, wv_ref, wo_ref, w_sems,
    q_s, k_s, v_s, dq_s, dk_s, dv_s, p_s, cs_s, dqa_s, dka_s, dm_s,
):
    rows, width = x_ref.shape
    length = rows // 2
    hd = width // HEADS
    scale = hd ** (-0.5)
    step = 256
    sources = (wq_hbm, wk_hbm, wv_hbm, wo_hbm)
    held = (wq_ref, wk_ref, wv_ref, wo_ref)
    cut = width // 2

    def start_load(i):
        for j in range(2):
            rows_of = pl.ds(j * cut, cut)
            pltpu.make_async_copy(
                sources[i].at[rows_of], held[i].at[rows_of], w_sems.at[2 * i + j]
            ).start()

    def wait_load(i):
        for j in range(2):
            rows_of = pl.ds(j * cut, cut)
            pltpu.make_async_copy(
                sources[i].at[rows_of], held[i].at[rows_of], w_sems.at[2 * i + j]
            ).wait()

    def project(weight, result):
        def body(n, carry):
            sl = pl.ds(pl.multiple_of(n * step, step), step)
            result[:, sl] = mm(x_ref[...], weight[:, sl]).astype(BF)
            return carry

        lax.fori_loop(0, width // step, body, 0)

    start_load(0)
    start_load(1)
    wait_load(0)
    project(wq_ref, q_s)
    wait_load(1)
    start_load(2)
    start_load(3)
    project(wk_ref, k_s)

    def window(h):
        first = (h * hd) // 128 * 128
        last = -(-(h * hd + hd) // 128) * 128
        return first, last

    def head_mask(h):
        first, last = window(h)
        lane = lax.broadcasted_iota(jnp.int32, (length, last - first), 1) + first
        return (lane >= h * hd) & (lane < h * hd + hd)

    def side(ref, s, first=0, last=width):
        return ref[s * length:(s + 1) * length, first:last]

    key_lane = lax.broadcasted_iota(jnp.int32, (length, length), 1)
    row_ids = lax.broadcasted_iota(jnp.int32, (length, 1), 0)
    for s in range(2):
        key_ok = key_lane < lens_ref[1 - s]
        live = (row_ids < lens_ref[s]).astype(F32)
        for h in range(HEADS):
            first, last = window(h)
            keys = side(k_s, 1 - s, first, last)
            keys = jnp.where(head_mask(h), keys, jnp.zeros_like(keys))
            scores = mm(side(q_s, s, first, last), keys, NT) * scale
            scores = jnp.where(key_ok, scores, -1000000000.0)
            expo = jnp.exp(scores - jnp.max(scores, axis=1, keepdims=True))
            probs = expo / jnp.sum(expo, axis=1, keepdims=True)
            p_s[s * HEADS + h] = probs
            rounded = probs.astype(BF).astype(F32)
            cs_s[s * HEADS + h:s * HEADS + h + 1, :] = jnp.sum(
                rounded * live, axis=0, keepdims=True
            )

    wait_load(2)
    project(wv_ref, v_s)
    wait_load(3)
    lane16 = lax.broadcasted_iota(jnp.int32, (HEADS, width), 1)
    head16 = lax.broadcasted_iota(jnp.int32, (HEADS, width), 0)
    own16 = (lane16 >= head16 * hd) & (lane16 < head16 * hd + hd)

    sum_x, ctx_sum, pieces = [], [], []
    for s in range(2):
        col_hi, col_lo = split(cs_s[s * HEADS:(s + 1) * HEADS, :], 2)
        other_v = side(v_s, 1 - s)
        full = mm(col_hi, other_v) + mm(col_lo, other_v)
        ctx = jnp.sum(jnp.where(own16, full, 0.0), axis=0, keepdims=True)
        ctx_sum.append(ctx)
        pieces += [part.astype(F32) for part in split(ctx, 3)]
        slot = lax.broadcasted_iota(jnp.int32, (8, length), 1)
        valid = (slot < lens_ref[s]).astype(F32).astype(BF)
        sum_x.append(mm(valid, side(x_ref, s))[0:1, :])
        other_x = side(x_ref, 1 - s)
        small_ref[s * HEADS:(s + 1) * HEADS, :] = (
            mm(col_hi, other_x) + mm(col_lo, other_x)
        ).astype(BF)
    zero = jnp.zeros((1, width), F32)
    stacked = jnp.concatenate(pieces + [zero, zero], axis=0).astype(BF)
    proj = mm(stacked, wo_ref[...])
    wc = wc_ref[...]
    pooled, lens = [], []
    for s in range(2):
        lens.append(jnp.full((1, 1), lens_ref[s], jnp.int32).astype(F32))
        out = proj[3 * s:3 * s + 1] + proj[3 * s + 1:3 * s + 2] + proj[3 * s + 2:3 * s + 3]
        pooled.append((sum_x[s] + out) / lens[s])
    logit = jnp.sum(wc * pooled[0] * pooled[1], axis=1, keepdims=True)
    label = jnp.full((1, 1), label_ref[0], jnp.int32).astype(F32)
    slope = 1.0 / (1.0 + jnp.exp(-logit)) - label
    d_mixed = [slope * wc * pooled[1 - s] / lens[s] for s in range(2)]
    d_rows = jnp.concatenate(d_mixed + [zero] * 6, axis=0)
    dm_s[...] = d_rows
    d_out = d_rows.astype(BF)
    d_ctx = mm(d_out, wo_ref[...], NT)
    tail = jnp.concatenate(
        ctx_sum + [d_out.astype(F32)[0:2], d_ctx[0:2], zero, zero], axis=0
    )
    small_ref[2 * HEADS:2 * HEADS + 8, :] = tail.astype(BF)

    dqa_s[...] = jnp.zeros_like(dqa_s)
    dka_s[...] = jnp.zeros_like(dka_s)
    for s in range(2):
        o = 1 - s
        grad = jnp.broadcast_to(d_ctx[s:s + 1], (HEADS, width))
        grad = jnp.where(own16, grad, 0.0).astype(BF)
        col_hi, col_lo = split(cs_s[s * HEADS:(s + 1) * HEADS, :], 2)
        dv_s[o * length:(o + 1) * length, :] = (
            mm(col_hi, grad, TN) + mm(col_lo, grad, TN)
        ).astype(BF)
        d_probs = mm(grad, side(v_s, o), NT).astype(BF).astype(F32)
        live = (row_ids < lens_ref[s]).astype(F32) * scale
        for h in range(HEADS):
            first, last = window(h)
            mask = head_mask(h)
            probs = p_s[s * HEADS + h]
            term = probs * d_probs[h:h + 1, :]
            total = jnp.sum(term, axis=1, keepdims=True)
            d_scores = ((term - probs * total) * live).astype(BF)
            keys = side(k_s, o, first, last)
            query = side(q_s, s, first, last)
            keys = jnp.where(mask, keys, jnp.zeros_like(keys))
            query = jnp.where(mask, query, jnp.zeros_like(query))
            dqa_s[s * length:(s + 1) * length, first:last] += mm(d_scores, keys)
            dka_s[o * length:(o + 1) * length, first:last] += mm(d_scores, query, TN)
    dq_s[...] = dqa_s[...].astype(BF)
    dk_s[...] = dka_s[...].astype(BF)

    @pl.when(core_ref[0] == 0)
    def _():
        own_ref[...] = dq_s[...]
        other_ref[...] = dk_s[...]

    @pl.when(core_ref[0] == 1)
    def _():
        own_ref[...] = dk_s[...]
        other_ref[...] = dq_s[...]

    def back(n, carry):
        sl = pl.ds(pl.multiple_of(n * step, step), step)
        total = mm(dq_s[...], wq_ref[sl, :], NT)
        total = total + mm(dk_s[...], wk_ref[sl, :], NT)
        total = total + mm(dv_s[...], wv_ref[sl, :], NT)
        for s in range(2):
            live = row_ids < lens_ref[s]
            mixed = jnp.where(live, dm_s[s:s + 1, sl], 0.0)
            din_ref[s * length:(s + 1) * length, sl] = (
                total[s * length:(s + 1) * length] + mixed
            ).astype(BF)
        return carry

    lax.fori_loop(0, width // step, back, 0)


def local_step(x, lens, label, core, wq, wk, wv, wo, wc):
    rows, width = x.shape
    length = rows // 2
    vmem = pl.BlockSpec(memory_space=pltpu.VMEM)
    smem = pl.BlockSpec(memory_space=pltpu.SMEM)
    like = jax.ShapeDtypeStruct((rows, width), BF)
    return pl.pallas_call(
        local_kernel,
        out_shape=(like, like, like, jax.ShapeDtypeStruct((2 * HEADS + 8, width), BF)),
        in_specs=[smem] * 3 + [vmem] + [pl.BlockSpec(memory_space=pl.ANY)] * 4 + [vmem],
        out_specs=(vmem,) * 4,
        scratch_shapes=[
            pltpu.VMEM((width, width), BF),
            pltpu.VMEM((width, width), BF),
            pltpu.VMEM((width, width), BF),
            pltpu.VMEM((width, width), BF),
            pltpu.SemaphoreType.DMA((8,)),
            pltpu.VMEM((rows, width), BF),
            pltpu.VMEM((rows, width), BF),
            pltpu.VMEM((rows, width), BF),
            pltpu.VMEM((rows, width), BF),
            pltpu.VMEM((rows, width), BF),
            pltpu.VMEM((rows, width), BF),
            pltpu.VMEM((2 * HEADS, length, length), F32),
            pltpu.VMEM((2 * HEADS, length), F32),
            pltpu.VMEM((rows, width), F32),
            pltpu.VMEM((rows, width), F32),
            pltpu.VMEM((8, width), F32),
        ],
        compiler_params=pltpu.CompilerParams(vmem_limit_bytes=56 * 1024 * 1024),
        cost_estimate=pl.CostEstimate(
            flops=6 * 2 * rows * width * width,
            bytes_accessed=4 * 2 * width * width + 8 * 2 * rows * width,
            transcendentals=2 * HEADS * length * length,
        ),
    )(lens, label, core.reshape(1), x, wq, wk, wv, wo, wc.reshape(1, width))


def swap(value, n, bit):
    return lax.ppermute(value, "dev", [(i, i ^ (1 << bit)) for i in range(n)])


def halve_step(part, me, n, bit, left):
    axis = left.index(bit)
    mine = (me >> bit) & 1
    keep = lax.dynamic_index_in_dim(part, mine, axis, keepdims=False)
    send = lax.dynamic_index_in_dim(part, 1 - mine, axis, keepdims=False)
    return keep, swap(send, n, bit), [b for b in left if b != bit]


def chain_sums(by_rows, slot_ids, chain_total):
    slots, row_block, width = by_rows.shape
    chain_index = jnp.arange(chain_total, dtype=jnp.int32)
    selector = (chain_index[:, None] == slot_ids[None, :]).astype(BF)
    summed = mm(selector, by_rows.reshape(slots, row_block * width)).astype(BF)
    return summed.reshape(chain_total, row_block, width)


def factor_grads(factors, me, n):
    width = factors.shape[2]
    block = width // n
    tail = 2 * HEADS
    column = jnp.arange(width, dtype=jnp.int32)[:, None]
    pick = (column == me * block + jnp.arange(block, dtype=jnp.int32)[None, :]).astype(BF)
    mine = mm(factors.reshape(-1, width), pick).astype(BF).reshape(n, -1, block)
    head_of = jnp.arange(width, dtype=jnp.int32) // (width // HEADS)
    own_head = head_of[None, :] == jnp.arange(HEADS, dtype=jnp.int32)[:, None]
    grads = factors[:, tail + 4:tail + 6]
    spread_grads = jnp.where(own_head, grads[:, :, None, :], jnp.zeros((), BF))
    d_wv = mm(
        mine[:, :tail].reshape(n * tail, block), spread_grads.reshape(n * tail, width), TN
    )
    d_wo = mm(
        mine[:, tail:tail + 2].reshape(n * 2, block),
        factors[:, tail + 2:tail + 4].reshape(n * 2, width),
        TN,
    )
    return d_wv, d_wo


def shards(n, embeddings, lengths, pairs, labels, w_query, w_key, w_value, w_out, w_class):
    length = embeddings.shape[1]
    width = embeddings.shape[2]
    chain_total = lengths.shape[0]
    me = lax.axis_index("dev")
    spread = lax.all_to_all(embeddings, "dev", split_axis=1, concat_axis=0, tiled=True)
    slot_ids = pairs.reshape(-1)
    picked = spread.at[slot_ids].get(mode="promise_in_bounds")
    gathered = lax.all_to_all(picked, "dev", split_axis=0, concat_axis=1, tiled=True)
    x = gathered.reshape(2 * length, width)
    my_pair = lax.dynamic_index_in_dim(pairs, me, 0, keepdims=False)
    chain_lens = lengths.at[my_pair].get(mode="promise_in_bounds")

    x_both = jnp.concatenate([x, swap(x, n, 0)], axis=0)
    core = me & 1
    first = core == 0
    d_input, own, other, small = local_step(
        x, chain_lens, labels, core, w_query, w_key, w_value, w_out, w_class
    )
    own_both = jnp.concatenate([own, swap(other, n, 0)], axis=0)
    factors = lax.all_gather(small, "dev", axis=0, tiled=False)
    slot_grads = d_input.reshape(2, length, width)
    by_rows = lax.all_to_all(slot_grads, "dev", split_axis=1, concat_axis=0, tiled=True)

    chips = n // 2
    block = width // n
    bits = chips.bit_length() - 1
    straight = list(range(1, bits + 1))
    crossed = list(straight)
    for i in range(0, bits - 1, 2):
        crossed[i], crossed[i + 1] = straight[i + 1], straight[i]
    orders = [straight, crossed]
    half = width // 2
    parts = [
        mm(x_both, own_both[:, i * half:(i + 1) * half], TN)
        .astype(BF)
        .reshape((2,) * bits + (2, block, half))
        for i in range(2)
    ]
    lefts = [straight[::-1]] * 2
    for turn in range(bits):
        kept, came = [], []
        for i in range(2):
            keep, got, lefts[i] = halve_step(parts[i], me, n, orders[i][turn], lefts[i])
            kept.append(keep)
            came.append(got)
        if turn == 0:
            summed = chain_sums(by_rows, slot_ids, chain_total)
            d_embeddings = lax.all_to_all(
                summed, "dev", split_axis=0, concat_axis=1, tiled=True
            )
            came[0], came[1], d_embeddings = lax.optimization_barrier(
                (came[0], came[1], d_embeddings)
            )
            d_embeddings = d_embeddings.astype(F32)
        elif turn == 1:
            came[0], came[1], d_embeddings = lax.optimization_barrier(
                (came[0], came[1], d_embeddings)
            )
            small_grads = factor_grads(factors, me, n)
        elif turn == 2:
            came[0], came[1], d_embeddings, small_grads = lax.optimization_barrier(
                (came[0], came[1], d_embeddings, small_grads)
            )
        else:
            came = list(lax.optimization_barrier(tuple(came)))
        parts = [k.astype(F32) + g.astype(F32) for k, g in zip(kept, came)]
        if turn < bits - 1:
            parts = [part.astype(BF) for part in parts]
    chip_sum = jnp.concatenate(parts, axis=-1)
    kept = lax.dynamic_index_in_dim(chip_sum, core, 0, keepdims=False)
    passed = lax.dynamic_index_in_dim(chip_sum, 1 - core, 0, keepdims=False)
    got = swap(passed.astype(BF), n, 0).astype(F32)
    d_wq = jnp.where(first, kept, got)
    d_wk = jnp.where(first, got, kept)

    d_weights = jnp.stack([d_wq, d_wk, small_grads[0], small_grads[1]], axis=1)
    return (d_embeddings, d_weights)


def solution(mesh):
    placed = (P("dev", None, None), P(), P(), P("dev"), P(), P(), P(), P(), P())
    return jax.shard_map(
        functools.partial(shards, mesh.shape["dev"]),
        mesh=mesh,
        in_specs=placed,
        out_specs=(P("dev", None, None), P("dev", None, None)),
        check_vma=False,
    )
```

```python
import functools

import jax
import jax.numpy as jnp
from jax import lax
from jax.experimental import pallas as pl
from jax.experimental.pallas import tpu as pltpu
from jax.sharding import PartitionSpec as P

HEADS = 16
BF = jnp.bfloat16
F32 = jnp.float32
NT = (((1,), (1,)), ((), ()))
TN = (((0,), (0,)), ((), ()))
NN = (((1,), (0,)), ((), ()))


def mm(a, b, dims=NN):
    return lax.dot_general(a, b, dims, preferred_element_type=F32)


def split(value, pieces):
    parts = []
    for _ in range(pieces):
        part = value.astype(BF)
        parts.append(part)
        value = value - part.astype(F32)
    return parts


def local_kernel(
    lens_ref, label_ref, core_ref, x_ref, wq_hbm, wk_hbm, wv_hbm, wo_hbm, wc_ref,
    din_ref, own_ref, other_ref, small_ref,
    wq_ref, wk_ref, wv_ref, wo_ref, w_sems,
    q_s, k_s, v_s, dq_s, dk_s, dv_s, p_s, cs_s, dqa_s, dka_s, dm_s,
):
    rows, width = x_ref.shape
    length = rows // 2
    hd = width // HEADS
    scale = hd ** (-0.5)
    step = 256
    sources = (wq_hbm, wk_hbm, wv_hbm, wo_hbm)
    held = (wq_ref, wk_ref, wv_ref, wo_ref)
    cut = width // 2

    def start_load(i):
        for j in range(2):
            rows_of = pl.ds(j * cut, cut)
            pltpu.make_async_copy(
                sources[i].at[rows_of], held[i].at[rows_of], w_sems.at[2 * i + j]
            ).start()

    def wait_load(i):
        for j in range(2):
            rows_of = pl.ds(j * cut, cut)
            pltpu.make_async_copy(
                sources[i].at[rows_of], held[i].at[rows_of], w_sems.at[2 * i + j]
            ).wait()

    def project(weight, result):
        def body(n, carry):
            sl = pl.ds(pl.multiple_of(n * step, step), step)
            result[:, sl] = mm(x_ref[...], weight[:, sl]).astype(BF)
            return carry

        lax.fori_loop(0, width // step, body, 0)

    start_load(0)
    start_load(1)
    wait_load(0)
    project(wq_ref, q_s)
    wait_load(1)
    start_load(2)
    start_load(3)
    project(wk_ref, k_s)

    def window(h):
        first = (h * hd) // 128 * 128
        last = -(-(h * hd + hd) // 128) * 128
        return first, last

    def head_mask(h):
        first, last = window(h)
        lane = lax.broadcasted_iota(jnp.int32, (length, last - first), 1) + first
        return (lane >= h * hd) & (lane < h * hd + hd)

    def side(ref, s, first=0, last=width):
        return ref[s * length:(s + 1) * length, first:last]

    key_lane = lax.broadcasted_iota(jnp.int32, (length, length), 1)
    row_ids = lax.broadcasted_iota(jnp.int32, (length, 1), 0)
    for s in range(2):
        key_ok = key_lane < lens_ref[1 - s]
        live = (row_ids < lens_ref[s]).astype(F32)
        for h in range(HEADS):
            first, last = window(h)
            keys = side(k_s, 1 - s, first, last)
            keys = jnp.where(head_mask(h), keys, jnp.zeros_like(keys))
            scores = mm(side(q_s, s, first, last), keys, NT) * scale
            scores = jnp.where(key_ok, scores, -1000000000.0)
            expo = jnp.exp(scores - jnp.max(scores, axis=1, keepdims=True))
            probs = expo / jnp.sum(expo, axis=1, keepdims=True)
            p_s[s * HEADS + h] = probs
            rounded = probs.astype(BF).astype(F32)
            cs_s[s * HEADS + h:s * HEADS + h + 1, :] = jnp.sum(
                rounded * live, axis=0, keepdims=True
            )

    wait_load(2)
    project(wv_ref, v_s)
    wait_load(3)
    lane16 = lax.broadcasted_iota(jnp.int32, (HEADS, width), 1)
    head16 = lax.broadcasted_iota(jnp.int32, (HEADS, width), 0)
    own16 = (lane16 >= head16 * hd) & (lane16 < head16 * hd + hd)

    sum_x, ctx_sum, pieces = [], [], []
    for s in range(2):
        col_hi, col_lo = split(cs_s[s * HEADS:(s + 1) * HEADS, :], 2)
        other_v = side(v_s, 1 - s)
        full = mm(col_hi, other_v) + mm(col_lo, other_v)
        ctx = jnp.sum(jnp.where(own16, full, 0.0), axis=0, keepdims=True)
        ctx_sum.append(ctx)
        pieces += [part.astype(F32) for part in split(ctx, 3)]
        slot = lax.broadcasted_iota(jnp.int32, (8, length), 1)
        valid = (slot < lens_ref[s]).astype(F32).astype(BF)
        sum_x.append(mm(valid, side(x_ref, s))[0:1, :])
        other_x = side(x_ref, 1 - s)
        small_ref[s * HEADS:(s + 1) * HEADS, :] = (
            mm(col_hi, other_x) + mm(col_lo, other_x)
        ).astype(BF)
    zero = jnp.zeros((1, width), F32)
    stacked = jnp.concatenate(pieces + [zero, zero], axis=0).astype(BF)
    proj = mm(stacked, wo_ref[...])
    wc = wc_ref[...]
    pooled, lens = [], []
    for s in range(2):
        lens.append(jnp.full((1, 1), lens_ref[s], jnp.int32).astype(F32))
        out = proj[3 * s:3 * s + 1] + proj[3 * s + 1:3 * s + 2] + proj[3 * s + 2:3 * s + 3]
        pooled.append((sum_x[s] + out) / lens[s])
    logit = jnp.sum(wc * pooled[0] * pooled[1], axis=1, keepdims=True)
    label = jnp.full((1, 1), label_ref[0], jnp.int32).astype(F32)
    slope = 1.0 / (1.0 + jnp.exp(-logit)) - label
    d_mixed = [slope * wc * pooled[1 - s] / lens[s] for s in range(2)]
    d_rows = jnp.concatenate(d_mixed + [zero] * 6, axis=0)
    dm_s[...] = d_rows
    d_out = d_rows.astype(BF)
    d_ctx = mm(d_out, wo_ref[...], NT)
    tail = jnp.concatenate(
        ctx_sum + [d_out.astype(F32)[0:2], d_ctx[0:2], zero, zero], axis=0
    )
    small_ref[2 * HEADS:2 * HEADS + 8, :] = tail.astype(BF)

    dqa_s[...] = jnp.zeros_like(dqa_s)
    dka_s[...] = jnp.zeros_like(dka_s)
    for s in range(2):
        o = 1 - s
        grad = jnp.broadcast_to(d_ctx[s:s + 1], (HEADS, width))
        grad = jnp.where(own16, grad, 0.0).astype(BF)
        col_hi, col_lo = split(cs_s[s * HEADS:(s + 1) * HEADS, :], 2)
        dv_s[o * length:(o + 1) * length, :] = (
            mm(col_hi, grad, TN) + mm(col_lo, grad, TN)
        ).astype(BF)
        d_probs = mm(grad, side(v_s, o), NT).astype(BF).astype(F32)
        live = (row_ids < lens_ref[s]).astype(F32) * scale
        for h in range(HEADS):
            first, last = window(h)
            mask = head_mask(h)
            probs = p_s[s * HEADS + h]
            term = probs * d_probs[h:h + 1, :]
            total = jnp.sum(term, axis=1, keepdims=True)
            d_scores = ((term - probs * total) * live).astype(BF)
            keys = side(k_s, o, first, last)
            query = side(q_s, s, first, last)
            keys = jnp.where(mask, keys, jnp.zeros_like(keys))
            query = jnp.where(mask, query, jnp.zeros_like(query))
            dqa_s[s * length:(s + 1) * length, first:last] += mm(d_scores, keys)
            dka_s[o * length:(o + 1) * length, first:last] += mm(d_scores, query, TN)
    dq_s[...] = dqa_s[...].astype(BF)
    dk_s[...] = dka_s[...].astype(BF)

    @pl.when(core_ref[0] == 0)
    def _():
        own_ref[...] = dq_s[...]
        other_ref[...] = dk_s[...]

    @pl.when(core_ref[0] == 1)
    def _():
        own_ref[...] = dk_s[...]
        other_ref[...] = dq_s[...]

    def back(n, carry):
        sl = pl.ds(pl.multiple_of(n * step, step), step)
        total = mm(dq_s[...], wq_ref[sl, :], NT)
        total = total + mm(dk_s[...], wk_ref[sl, :], NT)
        total = total + mm(dv_s[...], wv_ref[sl, :], NT)
        for s in range(2):
            live = row_ids < lens_ref[s]
            mixed = jnp.where(live, dm_s[s:s + 1, sl], 0.0)
            din_ref[s * length:(s + 1) * length, sl] = (
                total[s * length:(s + 1) * length] + mixed
            ).astype(BF)
        return carry

    lax.fori_loop(0, width // step, back, 0)


def local_step(x, lens, label, core, wq, wk, wv, wo, wc):
    rows, width = x.shape
    length = rows // 2
    vmem = pl.BlockSpec(memory_space=pltpu.VMEM)
    smem = pl.BlockSpec(memory_space=pltpu.SMEM)
    like = jax.ShapeDtypeStruct((rows, width), BF)
    return pl.pallas_call(
        local_kernel,
        out_shape=(like, like, like, jax.ShapeDtypeStruct((2 * HEADS + 8, width), BF)),
        in_specs=[smem] * 3 + [vmem] + [pl.BlockSpec(memory_space=pl.ANY)] * 4 + [vmem],
        out_specs=(vmem,) * 4,
        scratch_shapes=[
            pltpu.VMEM((width, width), BF),
            pltpu.VMEM((width, width), BF),
            pltpu.VMEM((width, width), BF),
            pltpu.VMEM((width, width), BF),
            pltpu.SemaphoreType.DMA((8,)),
            pltpu.VMEM((rows, width), BF),
            pltpu.VMEM((rows, width), BF),
            pltpu.VMEM((rows, width), BF),
            pltpu.VMEM((rows, width), BF),
            pltpu.VMEM((rows, width), BF),
            pltpu.VMEM((rows, width), BF),
            pltpu.VMEM((2 * HEADS, length, length), F32),
            pltpu.VMEM((2 * HEADS, length), F32),
            pltpu.VMEM((rows, width), F32),
            pltpu.VMEM((rows, width), F32),
            pltpu.VMEM((8, width), F32),
        ],
        compiler_params=pltpu.CompilerParams(vmem_limit_bytes=56 * 1024 * 1024),
        cost_estimate=pl.CostEstimate(
            flops=6 * 2 * rows * width * width,
            bytes_accessed=4 * 2 * width * width + 8 * 2 * rows * width,
            transcendentals=2 * HEADS * length * length,
        ),
    )(lens, label, core.reshape(1), x, wq, wk, wv, wo, wc.reshape(1, width))


def swap(value, n, bit):
    return lax.ppermute(value, "dev", [(i, i ^ (1 << bit)) for i in range(n)])


def halve_step(part, me, n, bit, left):
    axis = left.index(bit)
    mine = (me >> bit) & 1
    keep = lax.dynamic_index_in_dim(part, mine, axis, keepdims=False)
    send = lax.dynamic_index_in_dim(part, 1 - mine, axis, keepdims=False)
    return keep, swap(send, n, bit), [b for b in left if b != bit]


def chain_sums(by_rows, slot_ids, chain_total):
    slots, row_block, width = by_rows.shape
    chain_index = jnp.arange(chain_total, dtype=jnp.int32)
    selector = (chain_index[:, None] == slot_ids[None, :]).astype(BF)
    summed = mm(selector, by_rows.reshape(slots, row_block * width)).astype(BF)
    return summed.reshape(chain_total, row_block, width)


def factor_grads(factors, me, n):
    width = factors.shape[2]
    block = width // n
    tail = 2 * HEADS
    column = jnp.arange(width, dtype=jnp.int32)[:, None]
    pick = (column == me * block + jnp.arange(block, dtype=jnp.int32)[None, :]).astype(BF)
    mine = mm(factors.reshape(-1, width), pick).astype(BF).reshape(n, -1, block)
    head_of = jnp.arange(width, dtype=jnp.int32) // (width // HEADS)
    own_head = head_of[None, :] == jnp.arange(HEADS, dtype=jnp.int32)[:, None]
    grads = factors[:, tail + 4:tail + 6]
    spread_grads = jnp.where(own_head, grads[:, :, None, :], jnp.zeros((), BF))
    d_wv = mm(
        mine[:, :tail].reshape(n * tail, block), spread_grads.reshape(n * tail, width), TN
    )
    d_wo = mm(
        mine[:, tail:tail + 2].reshape(n * 2, block),
        factors[:, tail + 2:tail + 4].reshape(n * 2, width),
        TN,
    )
    return d_wv, d_wo


def shards(n, embeddings, lengths, pairs, labels, w_query, w_key, w_value, w_out, w_class):
    length = embeddings.shape[1]
    width = embeddings.shape[2]
    chain_total = lengths.shape[0]
    me = lax.axis_index("dev")
    spread = lax.all_to_all(embeddings, "dev", split_axis=1, concat_axis=0, tiled=True)
    slot_ids = pairs.reshape(-1)
    picked = spread.at[slot_ids].get(mode="promise_in_bounds")
    gathered = lax.all_to_all(picked, "dev", split_axis=0, concat_axis=1, tiled=True)
    x = gathered.reshape(2 * length, width)
    my_pair = lax.dynamic_index_in_dim(pairs, me, 0, keepdims=False)
    chain_lens = lengths.at[my_pair].get(mode="promise_in_bounds")

    x_both = jnp.concatenate([x, swap(x, n, 0)], axis=0)
    core = me & 1
    first = core == 0
    d_input, own, other, small = local_step(
        x, chain_lens, labels, core, w_query, w_key, w_value, w_out, w_class
    )
    own_both = jnp.concatenate([own, swap(other, n, 0)], axis=0)
    factors = lax.all_gather(small, "dev", axis=0, tiled=False)
    slot_grads = d_input.reshape(2, length, width)
    by_rows = lax.all_to_all(slot_grads, "dev", split_axis=1, concat_axis=0, tiled=True)

    chips = n // 2
    block = width // n
    bits = chips.bit_length() - 1
    straight = list(range(1, bits + 1))
    crossed = list(straight)
    for i in range(0, bits - 1, 2):
        crossed[i], crossed[i + 1] = straight[i + 1], straight[i]
    orders = [straight, crossed]
    half = width // 2
    parts = [
        mm(x_both, own_both[:, i * half:(i + 1) * half], TN)
        .astype(BF)
        .reshape((2,) * bits + (2, block, half))
        for i in range(2)
    ]
    lefts = [straight[::-1]] * 2
    for turn in range(bits):
        kept, came = [], []
        for i in range(2):
            keep, got, lefts[i] = halve_step(parts[i], me, n, orders[i][turn], lefts[i])
            kept.append(keep)
            came.append(got)
        if turn == 0:
            summed = chain_sums(by_rows, slot_ids, chain_total)
            d_embeddings = lax.all_to_all(
                summed, "dev", split_axis=0, concat_axis=1, tiled=True
            )
            came = list(lax.optimization_barrier(tuple(came)))
        elif turn == 1:
            came[0], came[1], d_embeddings = lax.optimization_barrier(
                (came[0], came[1], d_embeddings)
            )
            d_embeddings = d_embeddings.astype(F32)
            small_grads = factor_grads(factors, me, n)
        elif turn == 2:
            came[0], came[1], d_embeddings, small_grads = lax.optimization_barrier(
                (came[0], came[1], d_embeddings, small_grads)
            )
        else:
            came = list(lax.optimization_barrier(tuple(came)))
        parts = [k.astype(F32) + g.astype(F32) for k, g in zip(kept, came)]
        if turn < bits - 1:
            parts = [part.astype(BF) for part in parts]
    chip_sum = jnp.concatenate(parts, axis=-1)
    kept = lax.dynamic_index_in_dim(chip_sum, core, 0, keepdims=False)
    passed = lax.dynamic_index_in_dim(chip_sum, 1 - core, 0, keepdims=False)
    got = swap(passed.astype(BF), n, 0).astype(F32)
    d_wq = jnp.where(first, kept, got)
    d_wk = jnp.where(first, got, kept)

    d_weights = jnp.stack([d_wq, d_wk, small_grads[0], small_grads[1]], axis=1)
    return (d_embeddings, d_weights)


def solution(mesh):
    placed = (P("dev", None, None), P(), P(), P("dev"), P(), P(), P(), P(), P())
    return jax.shard_map(
        functools.partial(shards, mesh.shape["dev"]),
        mesh=mesh,
        in_specs=placed,
        out_specs=(P("dev", None, None), P("dev", None, None)),
        check_vma=False,
    )
```
